128 devices in a mesh: wide: 16 (over z, x), narrow: 8 (over y, core).
Axes of the slice: x: 4, y: 4, z: 4, core: 2. Of those that a mesh axis runs over, the one named last changes fastest.
Arguments:
- points: bfloat16 [131072, 1024], P(('wide', 'narrow')), may hold values from -8 to 8
- block_bucket: int32 [65536], P(('wide', 'narrow')), may hold values from 0 to 511, as said below
- fine: bfloat16 [262144, 1024], P(('wide', 'narrow')), may hold values from -8 to 8
- sharp: float32 [512], P(('wide', 'narrow')), may hold values from 0.5 to 4
- parents: int32 [262144], P(('wide', 'narrow')), may hold values from 0 to 4095, as said below
- coarse_old: bfloat16 [4096, 1024], P(('wide', 'narrow')), may hold values from -6 to 6
Outputs:
- fine_new: bfloat16 [262144, 1024], P(('wide', 'narrow'))
- coarse_new: bfloat16 [4096, 1024], P(('wide', 'narrow'))
- point_entropy: float32 [131072], P(('wide', 'narrow'))
The draws below stay inside these ranges and needn't reach their ends.
Inputs may be any that keep to these rules, and one draw needn't show every extreme that they name: `block_bucket`: among the 512 blocks of one device no bucket is named more than 2 times, and one bucket is named exactly 2 times by the blocks of every device. `parents`: the parent of fine centroid j is one of the 256 coarse centroids from (j // 16384) * 256 on.
All inputs are finite; a program needn't handle non-finite values.
Results may differ from the reference program's by a relative error of at most 0.0085.
Values may be sent and summed in bfloat16 or wider, within the bound.
A program may use at most 128 MiB of HBM per device.

```python
import math
import jax
import jax.numpy as jnp
from jax import lax

D = 1024
BUCKET = 512
CAP = 2
PB = 2
OWNERS = 128
TOTAL_BUCKETS = 512
BLK_DEV = 512
BLOCKS = 65536
POINTS = 131072
FINE = 262144
FINE_GROUP = 16384
GROUP_COARSE = 256
COARSE = 4096


def draw_block_bucket(key, part):
    key = jax.random.fold_in(key, 11)
    key_reward, key_popular, key_providers = jax.random.split(key, 3)
    reward_amount = jax.random.randint(key_reward, (TOTAL_BUCKETS,), 0, 4)
    popular_bucket = jax.random.randint(key_popular, (), 0, TOTAL_BUCKETS)
    bucket_numbers = jnp.arange(TOTAL_BUCKETS, dtype=jnp.int32)
    precedence = reward_amount + 64 * (bucket_numbers == popular_bucket).astype(jnp.int32)

    def one_source(source):
        source_key = jax.random.fold_in(key_providers, source)
        key_noise, key_shuffle = jax.random.split(source_key)
        jitter = jax.random.randint(key_noise, (TOTAL_BUCKETS,), 0, 16384)
        scores = (precedence * 16384 + jitter) * TOTAL_BUCKETS + bucket_numbers
        ranked = jnp.argsort(-scores)
        positions = jnp.arange(BLK_DEV, dtype=jnp.int32)
        half_blocks = BLK_DEV // 2
        quarter_buckets = TOTAL_BUCKETS // 4
        picked = jnp.where(positions < half_blocks, positions // 2, quarter_buckets + positions - half_blocks)
        chosen = ranked[picked].astype(jnp.int32)
        return jax.random.permutation(key_shuffle, chosen)
    table = jax.vmap(one_source)(jnp.arange(OWNERS, dtype=jnp.int32))
    return table.reshape(BLOCKS).astype(jnp.int32)


def draw_parents(key, part):
    key = jax.random.fold_in(key, 12)
    group_index = jnp.arange(FINE, dtype=jnp.int32) // FINE_GROUP
    offsets = jax.random.randint(key, (FINE,), 0, GROUP_COARSE)
    return (group_index * GROUP_COARSE + offsets).astype(jnp.int32)


def draw_fine(key, part):
    key = jax.random.fold_in(key, 13)
    key_values = jax.random.fold_in(key, 0)
    values = jax.random.truncated_normal(key_values, -6.0, 6.0, (FINE, D), jnp.float32)
    return values.astype(jnp.bfloat16)


def draw_points(key, part):
    key = jax.random.fold_in(key, 14)
    key_values = jax.random.fold_in(key, 0)
    values = jax.random.truncated_normal(key_values, -6.0, 6.0, (POINTS, D), jnp.float32)
    return values.astype(jnp.bfloat16)


def block_levels(stream_key, shape, pieces, low, top_value):
    loudness, own = 1.0, jax.random.fold_in(stream_key, 6)
    for axis_at, blocks in pieces:
        steps = jnp.exp(jax.random.uniform(jax.random.fold_in(own, axis_at), (blocks,), jnp.float32, low / len(pieces), top_value / len(pieces)))
        loudness = loudness * jnp.repeat(steps, shape[axis_at] // blocks).reshape([-1 if axis == axis_at else 1 for axis in range(len(shape))])
    return loudness


def gaussian(rng, dims, deviation, limit, shards=(), held_as=jnp.bfloat16):
    values = jax.random.normal(rng, dims, jnp.float32) * deviation
    if len(shards) > 0:
        values = block_levels(rng, dims, shards, -0.22, 0.18) * values
    return jnp.clip(values, min=-limit, max=limit).astype(held_as)


def setup_inputs(seed: int = 0) -> dict:
    key_of = jax.random.split(jax.random.key(seed), 7)
    points = draw_points(jax.random.fold_in(key_of[6], 71), 0)
    block_bucket = draw_block_bucket(jax.random.fold_in(key_of[6], 71), 0)
    fine = draw_fine(jax.random.fold_in(key_of[6], 71), 0)
    sharp = jnp.clip(jnp.exp(math.log(4.0) - 2.0794415 * jax.random.uniform(key_of[3], (TOTAL_BUCKETS,), jnp.float32) ** block_levels(key_of[3], (TOTAL_BUCKETS,), ((0, 128),), -0.2, 0.2)), 0.5, 4.0)
    parents = draw_parents(jax.random.fold_in(key_of[6], 71), 0)
    coarse_old = gaussian(key_of[5], (COARSE, D), 1.0, 6.0, ((0, 128),))
    return dict(points=points, block_bucket=block_bucket, fine=fine, sharp=sharp, parents=parents, coarse_old=coarse_old)


PRIOR_MASS = 1.0


def assign(row_data, row_live, centroids, sharpness):
    products = jnp.dot(row_data, centroids.T, preferred_element_type=jnp.float32)
    cent_float = centroids.astype(jnp.float32)
    sq_norms = jnp.sum(cent_float * cent_float, axis=1)
    logits = sharpness * (products - 0.5 * sq_norms[None, :]) * (D ** -0.5)
    highest = jnp.max(logits, axis=1, keepdims=True)
    shifted = logits - highest
    exponent = jnp.exp(shifted)
    totals = jnp.sum(exponent, axis=1, keepdims=True)
    probability = exponent / totals
    entropy = jnp.log(totals[:, 0]) - jnp.sum(probability * shifted, axis=1)
    weights = (probability * row_live[:, None]).astype(jnp.bfloat16)
    masses = jnp.sum(weights.astype(jnp.float32), axis=0)
    weighted = jnp.dot(weights.T, row_data, preferred_element_type=jnp.float32)
    return entropy, masses, weighted


def reference(points, block_bucket, fine, sharp, parents, coarse_old):
    bucket_table = block_bucket.reshape(OWNERS, BLK_DEV).astype(jnp.int32)
    positions = jnp.arange(BLK_DEV, dtype=jnp.int32)

    def rank_row(bucket_row):
        matching = bucket_row[:, None] == bucket_row[None, :]
        earlier = positions[None, :] < positions[:, None]
        return jnp.sum(matching & earlier, axis=1).astype(jnp.int32)

    ranking = lax.map(rank_row, bucket_table)
    sources = jnp.broadcast_to(jnp.arange(OWNERS, dtype=jnp.int32)[:, None], (OWNERS, BLK_DEV))
    block_ids = (sources * BLK_DEV + positions[None, :]).astype(jnp.int32)
    slot_table = jnp.full((TOTAL_BUCKETS, OWNERS, CAP), -1, dtype=jnp.int32).at[bucket_table, sources, ranking].set(block_ids)
    blocks = points.reshape(BLOCKS, PB, D)
    parent_sets = parents.reshape(TOTAL_BUCKETS, BUCKET)

    def visit_bucket(running, bucket):
        coarse_sum, coarse_mass = running
        filled = slot_table[bucket].reshape(OWNERS * CAP)
        slot_live = filled >= 0
        row_data = blocks[jnp.maximum(filled, 0)].reshape(OWNERS * CAP * PB, D)
        row_live = jnp.repeat(slot_live.astype(jnp.float32), PB)
        centroids = lax.dynamic_slice_in_dim(fine, (bucket * BUCKET).astype(jnp.int32), BUCKET, 0)
        entropy, masses, weighted = assign(row_data, row_live, centroids, sharp[bucket])
        numerator = weighted + PRIOR_MASS * centroids.astype(jnp.float32)
        updated = (numerator / (masses + PRIOR_MASS)[:, None]).astype(jnp.bfloat16)
        coarse_sum = coarse_sum.at[parent_sets[bucket]].add(numerator)
        coarse_mass = coarse_mass.at[parent_sets[bucket]].add(masses + PRIOR_MASS)
        return (coarse_sum, coarse_mass), (updated, entropy)

    initial = (jnp.zeros((COARSE, D), jnp.float32), jnp.zeros((COARSE,), jnp.float32))
    (coarse_sum, coarse_mass), (updated, entropy) = lax.scan(visit_bucket, initial, jnp.arange(TOTAL_BUCKETS, dtype=jnp.int32))
    fine_new = updated.reshape(FINE, D)
    entropy = entropy.reshape(TOTAL_BUCKETS, OWNERS, CAP, PB)
    point_entropy = entropy[bucket_table, sources, ranking].reshape(POINTS)
    coarse_new = (0.5 * coarse_old.astype(jnp.float32) + 0.5 * coarse_sum / (coarse_mass + PRIOR_MASS)[:, None]).astype(jnp.bfloat16)
    return fine_new, coarse_new, point_entropy
```

```python
import functools

import jax
import jax.numpy as jnp
from jax import lax
from jax.experimental import pallas as pl
from jax.experimental.pallas import tpu as pltpu
from jax.sharding import PartitionSpec as P

MESH = pl.DeviceIdType.MESH
F32 = jnp.float32
BF16 = jnp.bfloat16

CAP = 2
PRIOR_MASS = 1.0
STRIDE = 37
DEAD_MARK = 16.0
EXTRA = 16


def iota(shape, axis):
    return lax.broadcasted_iota(jnp.int32, shape, axis)


def dot(a, b, ca=1, cb=0):
    return lax.dot_general(a, b, (((ca,), (cb,)), ((), ())), preferred_element_type=F32)


def split(value):
    high = value.astype(BF16)
    return high, (value - high.astype(F32)).astype(BF16)


def kernel(
    dims,
    sharp_ref,
    bucket_ref,
    parent_hbm,
    points_hbm,
    fine_hbm,
    old_hbm,
    fine_out,
    coarse_out,
    entropy_out,
    points,
    cent,
    half_norm,
    parent,
    old,
    code,
    place,
    src,
    dst,
    numer,
    mass,
    staged,
    coarse,
    coarse_mass,
    ent,
    ret,
    core_send,
    core_recv,
    y_send,
    y_recv,
    load_sem,
    cent_sem,
    send_sem,
    recv_sem,
    ent_send_sem,
    ent_recv_sem,
    out_sem,
    core_sem,
    y_send_sem,
    y_recv_sem,
):
    wide, narrow = dims
    owners = wide * narrow
    buckets, _, block_slots, width = src.shape
    slot_rows = owners * block_slots
    size = half_norm.shape[1]
    n_points = points.shape[0]
    group = coarse.shape[0]
    inverse = pow(STRIDE, -1, owners)
    w, n = lax.axis_index("wide"), lax.axis_index("narrow")
    me = w * narrow + n

    def device(i):
        t = lax.rem(me + STRIDE * i, owners)
        return (t // narrow, lax.rem(t, narrow))

    def source(i):
        t = lax.rem(me + (owners - STRIDE) * i, owners)
        return (t // narrow, lax.rem(t, narrow))

    points_copy = pltpu.make_async_copy(points_hbm, points, load_sem.at[0])
    points_copy.start()
    barrier = pltpu.get_barrier_semaphore()

    @pl.loop(1, owners)
    def _(i):
        pl.semaphore_signal(barrier, inc=1, device_id=device(i), device_id_type=MESH)

    parent_copy = pltpu.make_async_copy(parent_hbm, parent, load_sem.at[1])
    parent_copy.start()
    old_copy = pltpu.make_async_copy(old_hbm, old, load_sem.at[2])
    old_copy.start()
    cent_copies = [
        pltpu.make_async_copy(
            fine_hbm.at[pl.ds(r * size, size)], cent.at[r, pl.ds(0, size)], cent_sem.at[r]
        )
        for r in range(buckets)
    ]
    for copy in cent_copies:
        copy.start()

    n_blocks = bucket_ref.shape[1]
    per_tile = 128 // 2
    column = jnp.transpose(jnp.broadcast_to(bucket_ref[...].astype(F32), (128, n_blocks)))
    lane = iota((1, 128), 1)
    for j in range(n_points // 128):
        own = column[per_tile * j : per_tile * (j + 1)]
        pick = iota((per_tile, 128), 0) == iota((per_tile, 128), 1) // 2
        name = jnp.sum(jnp.where(pick, own, 0.0), axis=0, keepdims=True)
        earlier = iota((n_blocks, 128), 0) < per_tile * j + iota((n_blocks, 128), 1) // 2
        rank = jnp.sum(jnp.where((column == name) & earlier, 1.0, 0.0), axis=0, keepdims=True)
        number = name.astype(jnp.int32)
        step = ((number // buckets - me) * inverse) & (owners - 1)
        tile = pl.ds(128 * j, 128)
        place[:, tile] = step
        code[:, tile] = (
            (number % buckets) * slot_rows
            + step * block_slots
            + rank.astype(jnp.int32) * (block_slots // CAP)
            + (lane & 1)
        )

    points_copy.wait()

    part = 256
    steps_in_part = part // block_slots

    def gather_part(r, c):
        base = r * slot_rows + c * part
        mask = code[...] - base == iota((part, n_points), 0)
        hot = jnp.where(mask, 1.0, 0.0)
        live = jnp.sum(hot, axis=1, keepdims=True)
        rows = dot(hot.astype(BF16), points[...])
        mark = jnp.where((iota((part, 128), 1) == 0) & (live < 0.5), DEAD_MARK, rows[:, :128])
        rows = jnp.concatenate([mark, rows[:, 128:]], axis=1).astype(BF16)
        src[r, pl.ds(c * steps_in_part, steps_in_part)] = rows.reshape(
            steps_in_part, block_slots, width
        )

    quarter = owners // 4

    def send_part(r, c):
        first = c * steps_in_part

        @pl.loop(first, first + steps_in_part)
        def _(i):
            @pl.when(i > 0)
            def _():
                pltpu.make_async_remote_copy(
                    src_ref=src.at[r, i],
                    dst_ref=dst.at[r, i],
                    send_sem=send_sem.at[r],
                    recv_sem=recv_sem.at[r, i // quarter],
                    device_id=device(i),
                    device_id_type=MESH,
                ).start()

    def send_own(r):
        pltpu.make_async_copy(src.at[r, 0], dst.at[r, 0], recv_sem.at[r, 0]).start()

    parts = slot_rows // part

    def send_bucket(r):
        @pl.loop(0, parts)
        def _(c):
            gather_part(r, c)
            send_part(r, c)

        send_own(r)

    def prepare(r):
        cent_copies[r].wait()
        corner = (iota((EXTRA, width), 0) == 0) & (iota((EXTRA, width), 1) == 0)
        cent[r, pl.ds(size, EXTRA)] = jnp.where(corner, 1.0, 0.0).astype(BF16)

        @pl.loop(0, size // 64)
        def _(b):
            rows = pl.ds(pl.multiple_of(b * 64, 64), 64)
            value = cent[r, rows].astype(F32)
            norm = jnp.sum(value * value, axis=1, keepdims=True)
            half_norm[r, rows] = jnp.broadcast_to(0.5 * norm, (64, 128))

    def assign(r, first, steps):
        rows = steps * block_slots
        for q in range(first // quarter, (first + steps) // quarter):
            landed = dst.at[r, pl.ds(q * quarter, quarter)]
            pltpu.make_async_copy(landed, landed, recv_sem.at[r, q]).wait()
        x = dst[r, pl.ds(first, steps)].reshape(rows, width)
        products = dot(cent[r], x, 1, 1)
        live = jnp.where(products[size : size + 1] < 0.75 * DEAD_MARK, 1.0, 0.0)
        norm = jnp.concatenate([half_norm[r]] * (rows // 128), axis=1)
        logits = (products[:size] - norm) * (sharp_ref[r] * width**-0.5)
        shifted = logits - jnp.max(logits, axis=0, keepdims=True)
        exponent = jnp.exp(shifted)
        total = jnp.sum(exponent, axis=0, keepdims=True)
        inverse_total = 1.0 / total
        entropy = jnp.log(total) - jnp.sum(exponent * shifted, axis=0, keepdims=True) * inverse_total
        for q in range(rows // 128):
            ent[r, first // quarter + q] = entropy[:, 128 * q : 128 * (q + 1)]

        @pl.loop(first, first + steps)
        def _(i):
            @pl.when(i > 0)
            def _():
                pltpu.make_async_remote_copy(
                    src_ref=ent.at[r, i // quarter],
                    dst_ref=ret.at[r, i],
                    send_sem=ent_send_sem.at[r],
                    recv_sem=ent_recv_sem.at[r],
                    device_id=source(i),
                    device_id_type=MESH,
                ).start()

        if first == 0:
            pltpu.make_async_copy(ent.at[r, 0], ret.at[r, 0], ent_recv_sem.at[r]).start()

        weights = (exponent * (inverse_total * live)).astype(BF16)
        weighed = dot(weights, jnp.ones((rows, 128), BF16))
        weighted = dot(weights, x)
        if first == 0:
            mass[...] = weighed + PRIOR_MASS
            numer[...] = weighted + PRIOR_MASS * cent[r, pl.ds(0, size)].astype(F32)
        else:
            mass[...] += weighed
            numer[...] += weighted

    def finish(r):
        own = parent[:, pl.ds(r * size, size)] - w * group
        member = jnp.where(own == iota((group, size), 0), 1.0, 0.0).astype(BF16)
        high, low = split(mass[...])
        part_mass = dot(member, high) + dot(member, low)
        part_sum = dot(member, numer[...].astype(BF16))
        if r == 0:
            coarse_mass[...] = part_mass
            coarse[...] = part_sum
        else:
            coarse_mass[...] += part_mass
            coarse[...] += part_sum

    def emit(r):
        if r >= 2:
            out_copy(r - 2).wait()
        scale = 1.0 / mass[...]
        for d in range(width // 128):
            cols = pl.ds(128 * d, 128)
            staged[r % 2, :, cols] = (numer[:, cols] * scale).astype(BF16)
        out_copy(r).start()

    def out_copy(r):
        return pltpu.make_async_copy(
            staged.at[r % 2], fine_out.at[pl.ds(r * size, size)], out_sem.at[r % 2]
        )

    def collect(r):
        pltpu.make_async_copy(ret.at[r], ret.at[r], ent_recv_sem.at[r]).wait()
        high, low = split(ret[r].reshape(owners, 128))
        hot = jnp.where(place[...] == iota((owners, n_points), 0), 1.0, 0.0).astype(BF16)
        found = dot(high, hot, 0, 0) + dot(low, hot, 0, 0)
        mine = (code[...] & 127) == iota((128, n_points), 0)
        mine = mine & (code[...] // slot_rows == r)
        value = jnp.sum(jnp.where(mine, found, 0.0), axis=0, keepdims=True)
        if r == 0:
            entropy_out[...] = value
        else:
            entropy_out[...] += value

    def whole_bucket(r):
        half = owners // 2
        assign(r, 0, half)
        assign(r, half, half)
        finish(r)
        emit(r)

    @pl.loop(0, parts)
    def _(c):
        gather_part(0, c)

    pl.semaphore_wait(barrier, owners - 1)

    @pl.loop(0, parts)
    def _(c):
        send_part(0, c)

    send_own(0)
    send_bucket(1)
    parent_copy.wait()
    prepare(0)
    send_bucket(2)
    whole_bucket(0)
    send_bucket(3)
    prepare(1)
    whole_bucket(1)
    collect(0)
    prepare(2)
    whole_bucket(2)
    collect(1)
    prepare(3)
    collect(2)
    for q in range(4):
        assign(3, q * quarter, quarter)
    finish(3)

    y, core = n // 2, lax.rem(n, 2)
    ys = narrow // 2
    own_rows = group // narrow

    def tile_of(value):
        high, low = split(value)
        return jnp.where(iota((own_rows, 128), 1) < 64, high.astype(F32), low.astype(F32))

    def whole_of(value):
        return value + pltpu.roll(value, 64, 1)

    for k in range(ys):
        rows = pl.ds(pl.multiple_of((2 * k + 1 - core) * own_rows, own_rows), own_rows)
        core_send[k, :, pl.ds(0, width)] = coarse[rows].astype(BF16)
        core_send[k, :, pl.ds(width, 128)] = tile_of(coarse_mass[rows]).astype(BF16)
    core_copy = pltpu.make_async_remote_copy(
        src_ref=core_send,
        dst_ref=core_recv,
        send_sem=core_sem.at[0],
        recv_sem=core_sem.at[1],
        device_id=(w, n + 1 - 2 * core),
        device_id_type=MESH,
    )
    core_copy.start()
    emit(3)
    core_copy.wait()

    def chip_sum(k):
        rows = pl.ds(pl.multiple_of((2 * k + core) * own_rows, own_rows), own_rows)
        total = coarse[rows] + core_recv[k, :, pl.ds(0, width)].astype(F32)
        weight = coarse_mass[rows] + whole_of(core_recv[k, :, pl.ds(width, 128)].astype(F32))
        return total, weight

    y_copies = []
    for k in range(1, ys):
        other = lax.rem(y + k, ys)
        total, weight = chip_sum(other)
        y_send[k - 1, :, pl.ds(0, width)] = total.astype(BF16)
        y_send[k - 1, :, pl.ds(width, 128)] = tile_of(weight).astype(BF16)
        copy = pltpu.make_async_remote_copy(
            src_ref=y_send.at[k - 1],
            dst_ref=y_recv.at[k - 1],
            send_sem=y_send_sem.at[k - 1],
            recv_sem=y_recv_sem.at[k - 1],
            device_id=(w, 2 * other + core),
            device_id_type=MESH,
        )
        copy.start()
        y_copies.append(copy)
    total, weight = chip_sum(y)
    old_copy.wait()
    collect(3)
    for k, copy in enumerate(y_copies):
        copy.wait()
        total = total + y_recv[k, :, pl.ds(0, width)].astype(F32)
        weight = weight + whole_of(y_recv[k, :, pl.ds(width, 128)].astype(F32))
    scale = 0.5 / (weight + PRIOR_MASS)
    for d in range(width // 128):
        cols = pl.ds(128 * d, 128)
        here = total[:, 128 * d : 128 * (d + 1)]
        coarse_out[:, cols] = (0.5 * old[:, cols].astype(F32) + here * scale).astype(BF16)

    for r in range(buckets):
        sent = src.at[r, pl.ds(0, owners - 1)]
        pltpu.make_async_copy(sent, sent, send_sem.at[r]).wait()
        sent = ret.at[r, pl.ds(0, owners - 1)]
        pltpu.make_async_copy(sent, sent, ent_send_sem.at[r]).wait()
    out_copy(2).wait()
    out_copy(3).wait()


def body(points, block_bucket, fine, sharp, parents, coarse_old):
    wide, narrow = lax.axis_size("wide"), lax.axis_size("narrow")
    owners = wide * narrow
    n_points, width = points.shape
    n_blocks = block_bucket.shape[0]
    buckets = sharp.shape[0]
    size = fine.shape[0] // buckets
    block_slots = CAP * (n_points // n_blocks)
    own_rows = coarse_old.shape[0]
    group = own_rows * narrow
    ys = narrow // 2
    whole = pl.BlockSpec(memory_space=pltpu.VMEM)
    anywhere = pl.BlockSpec(memory_space=pl.ANY)
    dma = pltpu.SemaphoreType.DMA
    fine_new, coarse_new, entropy = pl.pallas_call(
        functools.partial(kernel, (wide, narrow)),
        out_shape=(
            jax.ShapeDtypeStruct(fine.shape, BF16),
            jax.ShapeDtypeStruct(coarse_old.shape, BF16),
            jax.ShapeDtypeStruct((1, n_points), F32),
        ),
        in_specs=[pl.BlockSpec(memory_space=pltpu.SMEM), whole] + [anywhere] * 4,
        out_specs=(anywhere, whole, whole),
        scratch_shapes=[
            pltpu.VMEM((n_points, width), BF16),
            pltpu.VMEM((buckets, size + EXTRA, width), BF16),
            pltpu.VMEM((buckets, size, 128), F32),
            pltpu.VMEM((1, buckets * size), jnp.int32),
            pltpu.VMEM((own_rows, width), BF16),
            pltpu.VMEM((1, n_points), jnp.int32),
            pltpu.VMEM((1, n_points), jnp.int32),
            pltpu.VMEM((buckets, owners, block_slots, width), BF16),
            pltpu.VMEM((buckets, owners, block_slots, width), BF16),
            pltpu.VMEM((size, width), F32),
            pltpu.VMEM((size, 128), F32),
            pltpu.VMEM((2, size, width), BF16),
            pltpu.VMEM((group, width), F32),
            pltpu.VMEM((group, 128), F32),
            pltpu.VMEM((buckets, 4, 1, 128), F32),
            pltpu.VMEM((buckets, owners, 1, 128), F32),
            pltpu.VMEM((ys, own_rows, width + 128), BF16),
            pltpu.VMEM((ys, own_rows, width + 128), BF16),
            pltpu.VMEM((ys - 1, own_rows, width + 128), BF16),
            pltpu.VMEM((ys - 1, own_rows, width + 128), BF16),
            dma((3,)),
            dma((buckets,)),
            dma((buckets,)),
            dma((buckets, 4)),
            dma((buckets,)),
            dma((buckets,)),
            dma((2,)),
            dma((2,)),
            dma((ys - 1,)),
            dma((ys - 1,)),
        ],
        compiler_params=pltpu.CompilerParams(
            collective_id=0, has_side_effects=True, vmem_limit_bytes=56 << 20
        ),
    )(
        sharp,
        block_bucket.reshape(1, n_blocks),
        parents.reshape(1, buckets * size),
        points,
        fine,
        coarse_old,
    )
    return fine_new, coarse_new, entropy.reshape(n_points)


def solution(mesh):
    both = ("wide", "narrow")
    return jax.shard_map(
        body,
        mesh=mesh,
        in_specs=(P(both, None), P(both), P(both, None), P(both), P(both), P(both, None)),
        out_specs=(P(both, None), P(both, None), P(both)),
        check_vma=False,
    )
```

```python
import functools

import jax
import jax.numpy as jnp
from jax import lax
from jax.experimental import pallas as pl
from jax.experimental.pallas import tpu as pltpu
from jax.sharding import PartitionSpec as P

MESH = pl.DeviceIdType.MESH
F32 = jnp.float32
BF16 = jnp.bfloat16

CAP = 2
PRIOR_MASS = 1.0
STRIDE = 37
DEAD_MARK = 16.0
EXTRA = 16


def iota(shape, axis):
    return lax.broadcasted_iota(jnp.int32, shape, axis)


def dot(a, b, ca=1, cb=0):
    return lax.dot_general(a, b, (((ca,), (cb,)), ((), ())), preferred_element_type=F32)


def split(value):
    high = value.astype(BF16)
    return high, (value - high.astype(F32)).astype(BF16)


def collect(found_in, code, place, mine_of):
    owners, n_points = found_in.shape[0], code.shape[1]
    high, low = split(found_in)
    hot = jnp.where(place == iota((owners, n_points), 0), 1.0, 0.0).astype(BF16)
    found = dot(high, hot, 0, 0) + dot(low, hot, 0, 0)
    mine = mine_of(iota((128, n_points), 0))
    return jnp.sum(jnp.where(mine, found, 0.0), axis=0, keepdims=True)


def kernel(
    dims,
    sharp_ref,
    bucket_ref,
    parent_hbm,
    points_hbm,
    fine_hbm,
    old_hbm,
    fine_out,
    coarse_out,
    entropy_out,
    code,
    back_out,
    points,
    cent,
    half_norm,
    parent,
    old,
    src,
    dst,
    numer,
    mass,
    coarse,
    coarse_mass,
    packed,
    packed_back,
    ent,
    back,
    core_send0,
    core_send1,
    core_recv0,
    core_recv1,
    y_send0,
    y_send1,
    y_recv0,
    y_recv1,
    load_sem,
    cent_sem,
    send_sem,
    recv_sem,
    ent_send_sem,
    ent_recv_sem,
    core_send_sem,
    core_recv_sem,
    y_send_sem,
    y_recv_sem,
):
    wide, narrow = dims
    owners = wide * narrow
    buckets, _, block_slots, width = src.shape
    slot_rows = owners * block_slots
    size = half_norm.shape[1]
    n_points = points.shape[0]
    group = coarse.shape[0]
    inverse = pow(STRIDE, -1, owners)
    quarter = owners // 4
    last = buckets - 1
    w, n = lax.axis_index("wide"), lax.axis_index("narrow")
    me = w * narrow + n

    def device(i):
        t = lax.rem(me + STRIDE * i, owners)
        return (lax.div(t, narrow), lax.rem(t, narrow))

    def source(i):
        t = lax.rem(me + (owners - STRIDE) * i, owners)
        return (lax.div(t, narrow), lax.rem(t, narrow))

    def each_step(first, stop, act):
        if first == 0:
            for i in range(1, 4):
                act(i)

        @pl.loop(max(first // 4, 1), stop // 4)
        def _(g):
            for u in range(4):
                act(4 * g + u)

    points_copy = pltpu.make_async_copy(points_hbm, points, load_sem.at[0])
    points_copy.start()
    barrier = pltpu.get_barrier_semaphore()
    each_step(
        0,
        owners,
        lambda i: pl.semaphore_signal(
            barrier, inc=1, device_id=device(i), device_id_type=MESH
        ),
    )
    parent_copy = pltpu.make_async_copy(parent_hbm, parent, load_sem.at[1])
    parent_copy.start()
    old_copy = pltpu.make_async_copy(old_hbm, old, load_sem.at[2])
    old_copy.start()
    cent_copies = [
        pltpu.make_async_copy(
            fine_hbm.at[pl.ds(r * size, size)], cent.at[r, pl.ds(0, size)], cent_sem.at[r]
        )
        for r in range(buckets)
    ]
    for copy in cent_copies:
        copy.start()

    n_blocks = bucket_ref.shape[1]
    per_tile = 128 // 2
    column = jnp.transpose(jnp.broadcast_to(bucket_ref[...].astype(F32), (128, n_blocks)))
    lane = iota((1, 128), 1)
    for j in range(n_points // 128):
        own = column[per_tile * j : per_tile * (j + 1)]
        pick = iota((per_tile, 128), 0) == iota((per_tile, 128), 1) // 2
        name = jnp.sum(jnp.where(pick, own, 0.0), axis=0, keepdims=True)
        earlier = iota((n_blocks, 128), 0) < per_tile * j + iota((n_blocks, 128), 1) // 2
        rank = jnp.sum(jnp.where((column == name) & earlier, 1.0, 0.0), axis=0, keepdims=True)
        number = name.astype(jnp.int32)
        step = ((number // buckets - me) * inverse) & (owners - 1)
        code[:, pl.ds(128 * j, 128)] = (
            (number % buckets) * slot_rows
            + step * block_slots
            + rank.astype(jnp.int32) * (block_slots // CAP)
            + (lane & 1)
        )

    points_copy.wait()

    part = 256
    parts = slot_rows // part
    steps_in_part = part // block_slots

    def gather_part(r, c):
        base = r * slot_rows + c * part
        mask = code[...] - base == iota((part, n_points), 0)
        hot = jnp.where(mask, 1.0, 0.0)
        live = jnp.sum(hot, axis=1, keepdims=True)
        rows = dot(hot.astype(BF16), points[...])
        mark = jnp.where((iota((part, 128), 1) == 0) & (live < 0.5), DEAD_MARK, rows[:, :128])
        rows = jnp.concatenate([mark, rows[:, 128:]], axis=1).astype(BF16)
        src[r, pl.ds(c * steps_in_part, steps_in_part)] = rows.reshape(
            steps_in_part, block_slots, width
        )

    def send_part(r, c):
        for q in range(4 // parts):
            first = c * steps_in_part + q * quarter
            each_step(
                first,
                first + quarter,
                lambda i: pltpu.make_async_remote_copy(
                    src_ref=src.at[r, i],
                    dst_ref=dst.at[r, i],
                    send_sem=send_sem.at[r],
                    recv_sem=recv_sem.at[r, first // quarter],
                    device_id=device(i),
                    device_id_type=MESH,
                ).start(),
            )
        if c == 0:
            pltpu.make_async_copy(src.at[r, 0], dst.at[r, 0], recv_sem.at[r, 0]).start()

    def prepare(r):
        cent_copies[r].wait()
        corner = (iota((EXTRA, width), 0) == 0) & (iota((EXTRA, width), 1) == 0)
        cent[r, pl.ds(size, EXTRA)] = jnp.where(corner, 1.0, 0.0).astype(BF16)

        @pl.loop(0, size // 64)
        def _(b):
            rows = pl.ds(pl.multiple_of(b * 64, 64), 64)
            value = cent[r, rows].astype(F32)
            norm = jnp.sum(value * value, axis=1, keepdims=True)
            half_norm[r, rows] = jnp.broadcast_to(0.5 * norm, (64, 128))

    def assign(r, first, steps):
        rows = steps * block_slots
        for q in range(first // quarter, (first + steps) // quarter):
            landed = dst.at[r, pl.ds(q * quarter, quarter)]
            pltpu.make_async_copy(landed, landed, recv_sem.at[r, q]).wait()
        x = dst[r, pl.ds(first, steps)].reshape(rows, width)
        products = dot(cent[r], x, 1, 1)
        live = jnp.where(products[size : size + 1] < 0.75 * DEAD_MARK, 1.0, 0.0)
        norm = jnp.concatenate([half_norm[r]] * (rows // 128), axis=1)
        logits = (products[:size] - norm) * (sharp_ref[r] * width**-0.5)
        shifted = logits - jnp.max(logits, axis=0, keepdims=True)
        exponent = jnp.exp(shifted)
        total = jnp.sum(exponent, axis=0, keepdims=True)
        inverse_total = 1.0 / total
        entropy = jnp.log(total) - jnp.sum(exponent * shifted, axis=0, keepdims=True) * inverse_total
        weights = (exponent * (inverse_total * live)).astype(BF16)
        return x, weights, entropy

    def pack(r, first, entropy):
        held = lane // 32 == r
        for q in range(entropy.shape[1] // 128):
            row = entropy[:, 128 * q : 128 * (q + 1)]
            for g in range(4):
                at = 4 * (first // quarter + q) + g
                turn = (32 * (r - g)) % 128
                moved = pltpu.roll(row, turn, 1) if turn else row
                if r == 0:
                    packed[at] = moved
                else:
                    packed[at] = jnp.where(held, moved, packed[at])

    def weigh(r, first, x, weights):
        weighed = dot(weights, jnp.ones((x.shape[0], 128), BF16))
        weighted = dot(weights, x)
        if first == 0:
            mass[...] = weighed + PRIOR_MASS
            numer[...] = weighted + PRIOR_MASS * cent[r, pl.ds(0, size)].astype(F32)
        else:
            mass[...] += weighed
            numer[...] += weighted

    def member_of(r):
        own = parent[:, pl.ds(r * size, size)] - w * group
        return jnp.where(own == iota((group, size), 0), 1.0, 0.0).astype(BF16)

    def finish(r):
        member = member_of(r)
        high, low = split(mass[...])
        part_mass = dot(member, high) + dot(member, low)
        part_sum = dot(member, numer[...].astype(BF16))
        if r == 0:
            coarse_mass[...] = part_mass
            coarse[...] = part_sum
        else:
            coarse_mass[...] += part_mass
            coarse[...] += part_sum

    def emit(r):
        scale = 1.0 / mass[...]
        for d in range(width // 128):
            cols = pl.ds(128 * d, 128)
            fine_out[pl.ds(r * size, size), cols] = (numer[:, cols] * scale).astype(BF16)

    def whole_bucket(r):
        half = owners // 2
        for first in (0, half):
            x, weights, entropy = assign(r, first, half)
            pack(r, first, entropy)
            weigh(r, first, x, weights)
        finish(r)
        emit(r)

    gather_part(0, 0)
    pl.semaphore_wait(barrier, owners - 1)
    send_part(0, 0)
    for c in range(1, parts):
        gather_part(0, c)
        send_part(0, c)
    for r in range(1, buckets):
        for c in range(parts):
            gather_part(r, c)
            send_part(r, c)
    parent_copy.wait()
    prepare(0)
    prepare(1)
    whole_bucket(0)
    prepare(2)
    whole_bucket(1)
    prepare(3)
    whole_bucket(2)
    each_step(
        0,
        owners,
        lambda i: pltpu.make_async_remote_copy(
            src_ref=packed.at[lax.div(i, 8)],
            dst_ref=packed_back.at[i],
            send_sem=ent_send_sem.at[0],
            recv_sem=ent_recv_sem.at[0],
            device_id=source(i),
            device_id_type=MESH,
        ).start(),
    )
    pltpu.make_async_copy(packed.at[0], packed_back.at[0], ent_recv_sem.at[0]).start()

    def send_entropy(q):
        each_step(
            q * quarter,
            (q + 1) * quarter,
            lambda i: pltpu.make_async_remote_copy(
                src_ref=ent.at[q],
                dst_ref=back.at[i],
                send_sem=ent_send_sem.at[1],
                recv_sem=ent_recv_sem.at[1],
                device_id=source(i),
                device_id_type=MESH,
            ).start(),
        )
        if q == 0:
            pltpu.make_async_copy(ent.at[0], back.at[0], ent_recv_sem.at[1]).start()

    for q in range(3):
        x, weights, entropy = assign(last, q * quarter, quarter)
        ent[q] = entropy
        send_entropy(q)
        weigh(last, q * quarter, x, weights)
    finish(last)
    pltpu.make_async_copy(packed_back, packed_back, ent_recv_sem.at[0]).wait()
    entropy_out[...] = collect(
        packed_back[...].reshape(owners, 128),
        code[...],
        lax.shift_right_logical(code[...] & (slot_rows - 1), 2),
        lambda row: (code[...] < last * slot_rows)
        & (row == 32 * lax.shift_right_logical(code[...], 9) + (code[...] & 31)),
    )

    x, weights, entropy = assign(last, 3 * quarter, quarter)
    ent[3] = entropy
    shares = dot(member_of(last), weights)
    coarse_mass[...] += jnp.sum(shares, axis=1, keepdims=True)
    shares = shares.astype(BF16)

    y, core = lax.div(n, 2), lax.rem(n, 2)
    ys = narrow // 2
    own_rows = group // narrow
    half = width // 2
    core_sends, core_recvs = (core_send0, core_send1), (core_recv0, core_recv1)
    y_sends, y_recvs = (y_send0, y_send1), (y_recv0, y_recv1)

    def tile_of(value):
        high, low = split(value)
        return jnp.where(iota((own_rows, 128), 1) < 64, high.astype(F32), low.astype(F32)).astype(BF16)

    def whole_of(value):
        value = value.astype(F32)
        return value + pltpu.roll(value, 64, 1)

    def rows_of(k, c):
        return pl.ds(pl.multiple_of((2 * k + c) * own_rows, own_rows), own_rows)

    core_copies = []
    for h in range(2):
        cols = pl.ds(h * half, half)
        coarse[:, cols] += dot(shares, x[:, h * half : (h + 1) * half])
        for k in range(ys):
            rows = rows_of(k, 1 - core)
            core_sends[h][k, :, pl.ds(0, half)] = coarse[rows, cols].astype(BF16)
            if h == 0:
                core_sends[h][k, :, pl.ds(half, 128)] = tile_of(coarse_mass[rows])
        copy = pltpu.make_async_remote_copy(
            src_ref=core_sends[h],
            dst_ref=core_recvs[h],
            send_sem=core_send_sem.at[h],
            recv_sem=core_recv_sem.at[h],
            device_id=(w, n + 1 - 2 * core),
            device_id_type=MESH,
        )
        copy.start()
        core_copies.append(copy)
    send_entropy(3)

    def chip_sum(h, k):
        cols = pl.ds(h * half, half)
        rows = rows_of(k, core)
        return coarse[rows, cols] + core_recvs[h][k, :, pl.ds(0, half)].astype(F32)

    def chip_mass(k):
        return coarse_mass[rows_of(k, core)] + whole_of(core_recv0[k, :, pl.ds(half, 128)])

    y_copies = []
    for h in range(2):
        core_copies[h].wait()
        for k in range(1, ys):
            other = lax.rem(y + k, ys)
            y_sends[h][k - 1, :, pl.ds(0, half)] = chip_sum(h, other).astype(BF16)
            if h == 0:
                y_sends[h][k - 1, :, pl.ds(half, 128)] = tile_of(chip_mass(other))
            copy = pltpu.make_async_remote_copy(
                src_ref=y_sends[h].at[k - 1],
                dst_ref=y_recvs[h].at[k - 1],
                send_sem=y_send_sem.at[h, k - 1],
                recv_sem=y_recv_sem.at[h, k - 1],
                device_id=(w, 2 * other + core),
                device_id_type=MESH,
            )
            copy.start()
            y_copies.append(copy)
    weigh(last, 3 * quarter, x, weights)
    emit(last)
    old_copy.wait()
    total = [chip_sum(h, y) for h in range(2)]
    weight = chip_mass(y)
    pltpu.make_async_copy(back, back, ent_recv_sem.at[1]).wait()
    back_out[...] = back[...].reshape(owners, 128)
    for h in range(2):
        for k in range(ys - 1):
            y_copies[h * (ys - 1) + k].wait()
            total[h] = total[h] + y_recvs[h][k, :, pl.ds(0, half)].astype(F32)
            if h == 0:
                weight = weight + whole_of(y_recv0[k, :, pl.ds(half, 128)])
        scale = 0.5 / (weight + PRIOR_MASS)
        for d in range(half // 128):
            cols = pl.ds(h * half + 128 * d, 128)
            here = total[h][:, 128 * d : 128 * (d + 1)]
            coarse_out[:, cols] = (0.5 * old[:, cols].astype(F32) + here * scale).astype(BF16)

    for r in range(buckets):
        sent = src.at[r, pl.ds(0, owners - 1)]
        pltpu.make_async_copy(sent, sent, send_sem.at[r]).wait()
    for k, ref in enumerate((packed_back, back)):
        sent = ref.at[pl.ds(0, owners - 1)]
        pltpu.make_async_copy(sent, sent, ent_send_sem.at[k]).wait()


def close(fine, coarse, entropy, code, back, fine_out, coarse_out, entropy_out, point, sem):
    copies = [
        pltpu.make_async_copy(fine, fine_out, sem.at[0]),
        pltpu.make_async_copy(coarse, coarse_out, sem.at[1]),
    ]
    for copy in copies:
        copy.start()
    held = back.shape[0] * 4
    number = code[...]
    point[...] = entropy[...] + collect(
        back[...],
        number,
        lax.shift_right_logical(number & (held - 1), 2),
        lambda row: (number >= 3 * held) & (row == (number & 127)),
    )
    copies.append(pltpu.make_async_copy(point, entropy_out, sem.at[2]))
    copies[2].start()
    for copy in copies:
        copy.wait()


def body(points, block_bucket, fine, sharp, parents, coarse_old):
    wide, narrow = lax.axis_size("wide"), lax.axis_size("narrow")
    owners = wide * narrow
    n_points, width = points.shape
    n_blocks = block_bucket.shape[0]
    buckets = sharp.shape[0]
    size = fine.shape[0] // buckets
    block_slots = CAP * (n_points // n_blocks)
    own_rows = coarse_old.shape[0]
    group = own_rows * narrow
    ys = narrow // 2
    half = width // 2
    whole = pl.BlockSpec(memory_space=pltpu.VMEM)
    anywhere = pl.BlockSpec(memory_space=pl.ANY)
    in_hbm = pl.BlockSpec(memory_space=pltpu.HBM)
    dma = pltpu.SemaphoreType.DMA
    held = pl.pallas_call(
        functools.partial(kernel, (wide, narrow)),
        out_shape=(
            pltpu.VMEM(fine.shape, BF16),
            pltpu.VMEM(coarse_old.shape, BF16),
            pltpu.VMEM((1, n_points), F32),
            pltpu.VMEM((1, n_points), jnp.int32),
            pltpu.VMEM((owners, 128), F32),
        ),
        in_specs=[pl.BlockSpec(memory_space=pltpu.SMEM), whole] + [in_hbm] * 4,
        out_specs=(whole,) * 5,
        scratch_shapes=[
            pltpu.VMEM((n_points, width), BF16),
            pltpu.VMEM((buckets, size + EXTRA, width), BF16),
            pltpu.VMEM((buckets, size, 128), F32),
            pltpu.VMEM((1, buckets * size), jnp.int32),
            pltpu.VMEM((own_rows, width), BF16),
            pltpu.VMEM((buckets, owners, block_slots, width), BF16),
            pltpu.VMEM((buckets, owners, block_slots, width), BF16),
            pltpu.VMEM((size, width), F32),
            pltpu.VMEM((size, 128), F32),
            pltpu.VMEM((group, width), F32),
            pltpu.VMEM((group, 128), F32),
            pltpu.VMEM((owners // 8, 1, 128), F32),
            pltpu.VMEM((owners, 1, 128), F32),
            pltpu.VMEM((4, 1, 128), F32),
            pltpu.VMEM((owners, 1, 128), F32),
            pltpu.VMEM((ys, own_rows, half + 128), BF16),
            pltpu.VMEM((ys, own_rows, half), BF16),
            pltpu.VMEM((ys, own_rows, half + 128), BF16),
            pltpu.VMEM((ys, own_rows, half), BF16),
            pltpu.VMEM((ys - 1, own_rows, half + 128), BF16),
            pltpu.VMEM((ys - 1, own_rows, half), BF16),
            pltpu.VMEM((ys - 1, own_rows, half + 128), BF16),
            pltpu.VMEM((ys - 1, own_rows, half), BF16),
            dma((3,)),
            dma((buckets,)),
            dma((buckets,)),
            dma((buckets, 4)),
            dma((2,)),
            dma((2,)),
            dma((2,)),
            dma((2,)),
            dma((2, ys - 1)),
            dma((2, ys - 1)),
        ],
        compiler_params=pltpu.CompilerParams(
            collective_id=0, has_side_effects=True, vmem_limit_bytes=48 << 20
        ),
    )(
        sharp,
        block_bucket.reshape(1, n_blocks),
        *[
            pltpu.with_memory_space_constraint(value, pltpu.HBM)
            for value in (parents.reshape(1, buckets * size), points, fine, coarse_old)
        ],
    )
    fine_new, coarse_new, entropy = pl.pallas_call(
        close,
        out_shape=(
            jax.ShapeDtypeStruct(fine.shape, BF16),
            jax.ShapeDtypeStruct(coarse_old.shape, BF16),
            jax.ShapeDtypeStruct((1, n_points), F32),
        ),
        in_specs=[whole] * 5,
        out_specs=(anywhere,) * 3,
        scratch_shapes=[pltpu.VMEM((1, n_points), F32), dma((3,))],
        compiler_params=pltpu.CompilerParams(vmem_limit_bytes=16 << 20),
    )(*[pltpu.with_memory_space_constraint(value, pltpu.VMEM) for value in held])
    return fine_new, coarse_new, entropy.reshape(n_points)


def solution(mesh):
    both = ("wide", "narrow")
    return jax.shard_map(
        body,
        mesh=mesh,
        in_specs=(P(both, None), P(both), P(both, None), P(both), P(both), P(both, None)),
        out_specs=(P(both, None), P(both, None), P(both)),
        check_vma=False,
    )
```

```python
import functools

import jax
import jax.numpy as jnp
from jax import lax
from jax.experimental import pallas as pl
from jax.experimental.pallas import tpu as pltpu
from jax.sharding import PartitionSpec as P

MESH = pl.DeviceIdType.MESH
F32 = jnp.float32
BF16 = jnp.bfloat16

CAP = 2
PRIOR_MASS = 1.0
STRIDE = 37
DEAD_MARK = 16.0
EXTRA = 16


def iota(shape, axis):
    return lax.broadcasted_iota(jnp.int32, shape, axis)


def dot(a, b, ca=1, cb=0):
    return lax.dot_general(a, b, (((ca,), (cb,)), ((), ())), preferred_element_type=F32)


def split(value):
    high = value.astype(BF16)
    return high, (value - high.astype(F32)).astype(BF16)


def kernel(
    dims,
    sharp_hbm,
    bucket_hbm,
    parent_hbm,
    points_hbm,
    fine_hbm,
    old_hbm,
    fine_out,
    coarse_out,
    entropy_out,
    sharp_ref,
    bucket_ref,
    code,
    points,
    cent,
    half_norm,
    parent,
    old,
    src,
    dst,
    numer,
    mass,
    coarse,
    coarse_mass,
    packed,
    back,
    core_send0,
    core_send1,
    core_recv0,
    core_recv1,
    y_send0,
    y_send1,
    y_recv0,
    y_recv1,
    load_sem,
    cent_sem,
    send_sem,
    recv_sem,
    ent_sem,
    core_send_sem,
    core_recv_sem,
    y_send_sem,
    y_recv_sem,
):
    wide, narrow = dims
    owners = wide * narrow
    buckets, _, block_slots, width = src.shape
    slot_rows = owners * block_slots
    size = half_norm.shape[1]
    n_points = points.shape[0]
    group = coarse.shape[0]
    inverse = pow(STRIDE, -1, owners)
    quarter = owners // 4
    last = buckets - 1
    w, n = lax.axis_index("wide"), lax.axis_index("narrow")
    me = w * narrow + n

    def device(i):
        t = lax.rem(me + STRIDE * i, owners)
        return (lax.div(t, narrow), lax.rem(t, narrow))

    def source(i):
        t = lax.rem(me + (owners - STRIDE) * i, owners)
        return (lax.div(t, narrow), lax.rem(t, narrow))

    def each_step(first, stop, act):
        if first == 0:
            for i in range(1, 4):
                act(i)

        @pl.loop(max(first // 4, 1), stop // 4)
        def _(g):
            for u in range(4):
                act(4 * g + u)

    bucket_copy = pltpu.make_async_copy(bucket_hbm, bucket_ref, load_sem.at[3])
    bucket_copy.start()
    points_copy = pltpu.make_async_copy(points_hbm, points, load_sem.at[0])
    points_copy.start()
    barrier = pltpu.get_barrier_semaphore()
    each_step(
        0,
        owners,
        lambda i: pl.semaphore_signal(
            barrier, inc=1, device_id=device(i), device_id_type=MESH
        ),
    )
    sharp_copy = pltpu.make_async_copy(sharp_hbm, sharp_ref, load_sem.at[4])
    sharp_copy.start()
    parent_copy = pltpu.make_async_copy(parent_hbm, parent, load_sem.at[1])
    parent_copy.start()
    old_copy = pltpu.make_async_copy(old_hbm, old, load_sem.at[2])
    old_copy.start()
    cent_copies = [
        pltpu.make_async_copy(
            fine_hbm.at[pl.ds(r * size, size)], cent.at[r, pl.ds(0, size)], cent_sem.at[r]
        )
        for r in range(buckets)
    ]
    for copy in cent_copies:
        copy.start()

    n_blocks = bucket_ref.shape[1]
    per_tile = 128 // 2
    bucket_copy.wait()
    column = jnp.transpose(jnp.broadcast_to(bucket_ref[...].astype(F32), (128, n_blocks)))
    lane = iota((1, 128), 1)
    for j in range(n_points // 128):
        own = column[per_tile * j : per_tile * (j + 1)]
        pick = iota((per_tile, 128), 0) == iota((per_tile, 128), 1) // 2
        name = jnp.sum(jnp.where(pick, own, 0.0), axis=0, keepdims=True)
        earlier = iota((n_blocks, 128), 0) < per_tile * j + iota((n_blocks, 128), 1) // 2
        rank = jnp.sum(jnp.where((column == name) & earlier, 1.0, 0.0), axis=0, keepdims=True)
        number = name.astype(jnp.int32)
        step = ((number // buckets - me) * inverse) & (owners - 1)
        code[:, pl.ds(128 * j, 128)] = (
            (number % buckets) * slot_rows
            + step * block_slots
            + rank.astype(jnp.int32) * (block_slots // CAP)
            + (lane & 1)
        )

    points_copy.wait()

    def gather_part(r, first, steps):
        rows = steps * block_slots
        mask = code[...] - (r * slot_rows + first * block_slots) == iota((rows, n_points), 0)
        hot = jnp.where(mask, 1.0, 0.0)
        live = jnp.sum(hot, axis=1, keepdims=True)
        found = dot(hot.astype(BF16), points[...])
        mark = jnp.where((iota((rows, 128), 1) == 0) & (live < 0.5), DEAD_MARK, found[:, :128])
        found = jnp.concatenate([mark, found[:, 128:]], axis=1).astype(BF16)
        src[r, pl.ds(first, steps)] = found.reshape(steps, block_slots, width)

    def send_part(r, q):
        each_step(
            q * quarter,
            (q + 1) * quarter,
            lambda i: pltpu.make_async_remote_copy(
                src_ref=src.at[r, i],
                dst_ref=dst.at[r, i],
                send_sem=send_sem.at[r],
                recv_sem=recv_sem.at[r, q],
                device_id=device(i),
                device_id_type=MESH,
            ).start(),
        )
        if q == 0:
            pltpu.make_async_copy(src.at[r, 0], dst.at[r, 0], recv_sem.at[r, 0]).start()

    def prepare(r):
        cent_copies[r].wait()
        corner = (iota((EXTRA, width), 0) == 0) & (iota((EXTRA, width), 1) == 0)
        cent[r, pl.ds(size, EXTRA)] = jnp.where(corner, 1.0, 0.0).astype(BF16)

        @pl.loop(0, size // 64)
        def _(b):
            rows = pl.ds(pl.multiple_of(b * 64, 64), 64)
            value = cent[r, rows].astype(F32)
            norm = jnp.sum(value * value, axis=1, keepdims=True)
            half_norm[r, rows] = jnp.broadcast_to(0.5 * norm, (64, 128))

    def assign(r, first, steps):
        rows = steps * block_slots
        for q in range(first // quarter, (first + steps) // quarter):
            landed = dst.at[r, pl.ds(q * quarter, quarter)]
            pltpu.make_async_copy(landed, landed, recv_sem.at[r, q]).wait()
        x = dst[r, pl.ds(first, steps)].reshape(rows, width)
        products = dot(cent[r], x, 1, 1)
        live = jnp.where(products[size : size + 1] < 0.75 * DEAD_MARK, 1.0, 0.0)
        norm = jnp.concatenate([half_norm[r]] * (rows // 128), axis=1)
        logits = (products[:size] - norm) * (sharp_ref[0, r] * width**-0.5)
        shifted = logits - jnp.max(logits, axis=0, keepdims=True)
        exponent = jnp.exp(shifted)
        total = jnp.sum(exponent, axis=0, keepdims=True)
        inverse_total = 1.0 / total
        entropy = jnp.log(total) - jnp.sum(exponent * shifted, axis=0, keepdims=True) * inverse_total
        weights = (exponent * (inverse_total * live)).astype(BF16)
        return x, weights, entropy

    def pack(r, first, entropy):
        held = lane // 32 == r
        for q in range(entropy.shape[1] // 128):
            row = entropy[:, 128 * q : 128 * (q + 1)]
            for g in range(4):
                at = 4 * (first // quarter + q) + g
                turn = (32 * (r - g)) % 128
                moved = pltpu.roll(row, turn, 1) if turn else row
                if r == 0:
                    packed[at] = moved
                else:
                    packed[at] = jnp.where(held, moved, packed[at])

    def weigh(r, first, x, weights):
        weighed = dot(weights, jnp.ones((x.shape[0], 128), BF16))
        weighted = dot(weights, x)
        if first == 0:
            mass[...] = weighed + PRIOR_MASS
            numer[...] = weighted + PRIOR_MASS * cent[r, pl.ds(0, size)].astype(F32)
        else:
            mass[...] += weighed
            numer[...] += weighted

    def member_of(r):
        own = parent[:, pl.ds(r * size, size)] - w * group
        return jnp.where(own == iota((group, size), 0), 1.0, 0.0).astype(BF16)

    def finish(r):
        member = member_of(r)
        high, low = split(mass[...])
        part_mass = dot(member, high) + dot(member, low)
        part_sum = dot(member, numer[...].astype(BF16))
        if r == 0:
            coarse_mass[...] = part_mass
            coarse[...] = part_sum
        else:
            coarse_mass[...] += part_mass
            coarse[...] += part_sum

    def emit(r):
        scale = 1.0 / mass[...]
        for d in range(width // 128):
            cols = pl.ds(128 * d, 128)
            fine_out[pl.ds(r * size, size), cols] = (numer[:, cols] * scale).astype(BF16)

    def whole_bucket(r):
        half = owners // 2
        for first in (0, half):
            x, weights, entropy = assign(r, first, half)
            pack(r, first, entropy)
            weigh(r, first, x, weights)
        finish(r)
        emit(r)

    gather_part(0, 0, quarter)
    pl.semaphore_wait(barrier, owners - 1)
    send_part(0, 0)
    for q in range(1, 4):
        gather_part(0, q * quarter, quarter)
        send_part(0, q)
    for r in range(1, buckets):
        for q in (0, 2):
            gather_part(r, q * quarter, 2 * quarter)
            send_part(r, q)
            send_part(r, q + 1)
    sharp_copy.wait()
    parent_copy.wait()
    prepare(0)
    prepare(1)
    whole_bucket(0)
    prepare(2)
    whole_bucket(1)
    prepare(3)
    whole_bucket(2)

    def send_entropy(q):
        each_step(
            q * quarter,
            (q + 1) * quarter,
            lambda i: pltpu.make_async_remote_copy(
                src_ref=packed.at[lax.div(i, 8)],
                dst_ref=back.at[i],
                send_sem=ent_sem.at[0],
                recv_sem=ent_sem.at[1],
                device_id=source(i),
                device_id_type=MESH,
            ).start(),
        )
        if q == 0:
            pltpu.make_async_copy(packed.at[0], back.at[0], ent_sem.at[1]).start()

    for q in range(3):
        x, weights, entropy = assign(last, q * quarter, quarter)
        pack(last, q * quarter, entropy)
        send_entropy(q)
        weigh(last, q * quarter, x, weights)
    finish(last)

    x, weights, entropy = assign(last, 3 * quarter, quarter)
    shares = dot(member_of(last), weights)
    coarse_mass[...] += jnp.sum(shares, axis=1, keepdims=True)
    shares = shares.astype(BF16)

    y, core = lax.div(n, 2), lax.rem(n, 2)
    ys = narrow // 2
    own_rows = group // narrow
    half = width // 2
    core_sends, core_recvs = (core_send0, core_send1), (core_recv0, core_recv1)
    y_sends, y_recvs = (y_send0, y_send1), (y_recv0, y_recv1)

    def tile_of(value):
        high, low = split(value)
        return jnp.where(iota((own_rows, 128), 1) < 64, high.astype(F32), low.astype(F32)).astype(BF16)

    def whole_of(value):
        value = value.astype(F32)
        return value + pltpu.roll(value, 64, 1)

    def rows_of(k, c):
        return pl.ds(pl.multiple_of((2 * k + c) * own_rows, own_rows), own_rows)

    core_copies = []
    for h in range(2):
        cols = pl.ds(h * half, half)
        coarse[:, cols] += dot(shares, x[:, h * half : (h + 1) * half])
        for k in range(ys):
            rows = rows_of(k, 1 - core)
            core_sends[h][k, :, pl.ds(0, half)] = coarse[rows, cols].astype(BF16)
            if h == 0:
                core_sends[h][k, :, pl.ds(half, 128)] = tile_of(coarse_mass[rows])
        copy = pltpu.make_async_remote_copy(
            src_ref=core_sends[h],
            dst_ref=core_recvs[h],
            send_sem=core_send_sem.at[h],
            recv_sem=core_recv_sem.at[h],
            device_id=(w, n + 1 - 2 * core),
            device_id_type=MESH,
        )
        copy.start()
        core_copies.append(copy)
    pack(last, 3 * quarter, entropy)
    send_entropy(3)

    def chip_sum(h, k):
        cols = pl.ds(h * half, half)
        rows = rows_of(k, core)
        return coarse[rows, cols] + core_recvs[h][k, :, pl.ds(0, half)].astype(F32)

    def chip_mass(k):
        return coarse_mass[rows_of(k, core)] + whole_of(core_recv0[k, :, pl.ds(half, 128)])

    y_copies = []
    for h in range(2):
        core_copies[h].wait()
        for k in range(1, ys):
            other = lax.rem(y + k, ys)
            y_sends[h][k - 1, :, pl.ds(0, half)] = chip_sum(h, other).astype(BF16)
            if h == 0:
                y_sends[h][k - 1, :, pl.ds(half, 128)] = tile_of(chip_mass(other))
            copy = pltpu.make_async_remote_copy(
                src_ref=y_sends[h].at[k - 1],
                dst_ref=y_recvs[h].at[k - 1],
                send_sem=y_send_sem.at[h, k - 1],
                recv_sem=y_recv_sem.at[h, k - 1],
                device_id=(w, 2 * other + core),
                device_id_type=MESH,
            )
            copy.start()
            y_copies.append(copy)
    weigh(last, 3 * quarter, x, weights)
    emit(last)
    old_copy.wait()
    total = [chip_sum(h, y) for h in range(2)]
    weight = chip_mass(y)
    pltpu.make_async_copy(back, back, ent_sem.at[1]).wait()
    high, low = split(back[...].reshape(owners, 128))
    number = code[...]
    place = lax.shift_right_logical(number & (slot_rows - 1), 2)
    hot = jnp.where(place == iota((owners, n_points), 0), 1.0, 0.0).astype(BF16)
    found = dot(high, hot, 0, 0) + dot(low, hot, 0, 0)
    spot = 32 * lax.shift_right_logical(number, 9) + (number & 31)
    mine = spot == iota((128, n_points), 0)
    entropy_out[...] = jnp.sum(jnp.where(mine, found, 0.0), axis=0, keepdims=True)
    for h in range(2):
        for k in range(ys - 1):
            y_copies[h * (ys - 1) + k].wait()
            total[h] = total[h] + y_recvs[h][k, :, pl.ds(0, half)].astype(F32)
            if h == 0:
                weight = weight + whole_of(y_recv0[k, :, pl.ds(half, 128)])
        scale = 0.5 / (weight + PRIOR_MASS)
        for d in range(half // 128):
            cols = pl.ds(h * half + 128 * d, 128)
            here = total[h][:, 128 * d : 128 * (d + 1)]
            coarse_out[:, cols] = (0.5 * old[:, cols].astype(F32) + here * scale).astype(BF16)

    for r in range(buckets):
        sent = src.at[r, pl.ds(0, owners - 1)]
        pltpu.make_async_copy(sent, sent, send_sem.at[r]).wait()
    sent = back.at[pl.ds(0, owners - 1)]
    pltpu.make_async_copy(sent, sent, ent_sem.at[0]).wait()


def close(fine, coarse, entropy, fine_out, coarse_out, entropy_out, sem):
    pieces = 8
    rows = fine.shape[0] // pieces
    copies = [
        pltpu.make_async_copy(
            fine.at[pl.ds(k * rows, rows)], fine_out.at[pl.ds(k * rows, rows)], sem.at[k]
        )
        for k in range(pieces)
    ]
    copies.append(pltpu.make_async_copy(coarse, coarse_out, sem.at[pieces]))
    copies.append(pltpu.make_async_copy(entropy, entropy_out, sem.at[pieces + 1]))
    for copy in copies:
        copy.start()
    for copy in copies:
        copy.wait()


def body(points, block_bucket, fine, sharp, parents, coarse_old):
    wide, narrow = lax.axis_size("wide"), lax.axis_size("narrow")
    owners = wide * narrow
    n_points, width = points.shape
    n_blocks = block_bucket.shape[0]
    buckets = sharp.shape[0]
    size = fine.shape[0] // buckets
    block_slots = CAP * (n_points // n_blocks)
    own_rows = coarse_old.shape[0]
    group = own_rows * narrow
    ys = narrow // 2
    half = width // 2
    whole = pl.BlockSpec(memory_space=pltpu.VMEM)
    anywhere = pl.BlockSpec(memory_space=pl.ANY)
    in_hbm = pl.BlockSpec(memory_space=pltpu.HBM)
    dma = pltpu.SemaphoreType.DMA
    held = pl.pallas_call(
        functools.partial(kernel, (wide, narrow)),
        out_shape=(
            pltpu.VMEM(fine.shape, BF16),
            pltpu.VMEM(coarse_old.shape, BF16),
            pltpu.VMEM((1, n_points), F32),
        ),
        in_specs=[in_hbm] * 6,
        out_specs=(whole,) * 3,
        scratch_shapes=[
            pltpu.SMEM((1, buckets), F32),
            pltpu.VMEM((1, n_blocks), jnp.int32),
            pltpu.VMEM((1, n_points), jnp.int32),
            pltpu.VMEM((n_points, width), BF16),
            pltpu.VMEM((buckets, size + EXTRA, width), BF16),
            pltpu.VMEM((buckets, size, 128), F32),
            pltpu.VMEM((1, buckets * size), jnp.int32),
            pltpu.VMEM((own_rows, width), BF16),
            pltpu.VMEM((buckets, owners, block_slots, width), BF16),
            pltpu.VMEM((buckets, owners, block_slots, width), BF16),
            pltpu.VMEM((size, width), F32),
            pltpu.VMEM((size, 128), F32),
            pltpu.VMEM((group, width), F32),
            pltpu.VMEM((group, 128), F32),
            pltpu.VMEM((owners // 8, 1, 128), F32),
            pltpu.VMEM((owners, 1, 128), F32),
            pltpu.VMEM((ys, own_rows, half + 128), BF16),
            pltpu.VMEM((ys, own_rows, half), BF16),
            pltpu.VMEM((ys, own_rows, half + 128), BF16),
            pltpu.VMEM((ys, own_rows, half), BF16),
            pltpu.VMEM((ys - 1, own_rows, half + 128), BF16),
            pltpu.VMEM((ys - 1, own_rows, half), BF16),
            pltpu.VMEM((ys - 1, own_rows, half + 128), BF16),
            pltpu.VMEM((ys - 1, own_rows, half), BF16),
            dma((5,)),
            dma((buckets,)),
            dma((buckets,)),
            dma((buckets, 4)),
            dma((2,)),
            dma((2,)),
            dma((2,)),
            dma((2, ys - 1)),
            dma((2, ys - 1)),
        ],
        compiler_params=pltpu.CompilerParams(
            collective_id=0, has_side_effects=True, vmem_limit_bytes=48 << 20
        ),
    )(
        *[
            pltpu.with_memory_space_constraint(value, pltpu.HBM)
            for value in (
                sharp.reshape(1, buckets),
                block_bucket.reshape(1, n_blocks),
                parents.reshape(1, buckets * size),
                points,
                fine,
                coarse_old,
            )
        ],
    )
    fine_new, coarse_new, entropy = pl.pallas_call(
        close,
        out_shape=(
            jax.ShapeDtypeStruct(fine.shape, BF16),
            jax.ShapeDtypeStruct(coarse_old.shape, BF16),
            jax.ShapeDtypeStruct((1, n_points), F32),
        ),
        in_specs=[whole] * 3,
        out_specs=(anywhere,) * 3,
        scratch_shapes=[dma((10,))],
        compiler_params=pltpu.CompilerParams(vmem_limit_bytes=16 << 20),
    )(*[pltpu.with_memory_space_constraint(value, pltpu.VMEM) for value in held])
    return fine_new, coarse_new, entropy.reshape(n_points)


def solution(mesh):
    both = ("wide", "narrow")
    return jax.shard_map(
        body,
        mesh=mesh,
        in_specs=(P(both, None), P(both), P(both, None), P(both), P(both), P(both, None)),
        out_specs=(P(both, None), P(both, None), P(both)),
        check_vma=False,
    )
```

```python
import functools

import jax
import jax.numpy as jnp
from jax import lax
from jax.experimental import pallas as pl
from jax.experimental.pallas import tpu as pltpu
from jax.sharding import PartitionSpec as P

MESH = pl.DeviceIdType.MESH
F32 = jnp.float32
BF16 = jnp.bfloat16

CAP = 2
PRIOR_MASS = 1.0
STRIDE = 91
DEAD_MARK = 16.0
EXTRA = 16


def iota(shape, axis):
    return lax.broadcasted_iota(jnp.int32, shape, axis)


def dot(a, b, ca=1, cb=0):
    return lax.dot_general(a, b, (((ca,), (cb,)), ((), ())), preferred_element_type=F32)


def split(value):
    high = value.astype(BF16)
    return high, (value - high.astype(F32)).astype(BF16)


def kernel(
    dims,
    sharp_hbm,
    bucket_hbm,
    parent_hbm,
    points_hbm,
    fine_hbm,
    fine_out,
    total_out,
    weight_out,
    code,
    back_out,
    sharp_ref,
    bucket_ref,
    points,
    cent,
    half_norm,
    parent,
    src,
    dst,
    numer,
    mass,
    coarse,
    coarse_mass,
    packed,
    back,
    core_send0,
    core_send1,
    core_recv0,
    core_recv1,
    y_send0,
    y_send1,
    y_recv0,
    y_recv1,
    load_sem,
    cent_sem,
    send_sem,
    recv_sem,
    ent_sem,
    core_send_sem,
    core_recv_sem,
    y_send_sem,
    y_recv_sem,
):
    wide, narrow = dims
    owners = wide * narrow
    buckets, _, block_slots, width = src.shape
    slot_rows = owners * block_slots
    size = half_norm.shape[1]
    n_points = points.shape[0]
    group = coarse.shape[0]
    inverse = pow(STRIDE, -1, owners)
    quarter = owners // 4
    last = buckets - 1
    w, n = lax.axis_index("wide"), lax.axis_index("narrow")
    me = w * narrow + n

    def device(i):
        t = lax.rem(me + STRIDE * i, owners)
        return (lax.div(t, narrow), lax.rem(t, narrow))

    def source(i):
        t = lax.rem(me + (owners - STRIDE) * i, owners)
        return (lax.div(t, narrow), lax.rem(t, narrow))

    def each_step(first, stop, act):
        if first == 0:
            for i in range(1, 4):
                act(i)

        @pl.loop(max(first // 4, 1), stop // 4)
        def _(g):
            for u in range(4):
                act(4 * g + u)

    bucket_copy = pltpu.make_async_copy(bucket_hbm, bucket_ref, load_sem.at[2])
    bucket_copy.start()
    points_copy = pltpu.make_async_copy(points_hbm, points, load_sem.at[0])
    points_copy.start()
    barrier = pltpu.get_barrier_semaphore()
    each_step(
        0,
        owners,
        lambda i: pl.semaphore_signal(
            barrier, inc=1, device_id=device(i), device_id_type=MESH
        ),
    )
    n_blocks = bucket_ref.shape[1]
    per_tile = 128 // 2
    bucket_copy.wait()
    column = jnp.transpose(jnp.broadcast_to(bucket_ref[...].astype(F32), (128, n_blocks)))
    lane = iota((1, 128), 1)
    for j in range(n_points // 128):
        own = column[per_tile * j : per_tile * (j + 1)]
        pick = iota((per_tile, 128), 0) == iota((per_tile, 128), 1) // 2
        name = jnp.sum(jnp.where(pick, own, 0.0), axis=0, keepdims=True)
        upto = per_tile * (j + 1)
        earlier = iota((upto, 128), 0) < per_tile * j + iota((upto, 128), 1) // 2
        same = (column[:upto] == name) & earlier
        rank = jnp.sum(jnp.where(same, 1.0, 0.0), axis=0, keepdims=True)
        number = name.astype(jnp.int32)
        step = ((number // buckets - me) * inverse) & (owners - 1)
        code[:, pl.ds(128 * j, 128)] = (
            (number % buckets) * slot_rows
            + step * block_slots
            + rank.astype(jnp.int32) * (block_slots // CAP)
            + (lane & 1)
        )

    points_copy.wait()

    def gather_part(r, first, steps):
        rows = steps * block_slots
        mask = code[...] - (r * slot_rows + first * block_slots) == iota((rows, n_points), 0)
        hot = jnp.where(mask, 1.0, 0.0)
        live = jnp.sum(hot, axis=1, keepdims=True)
        found = dot(hot.astype(BF16), points[...])
        mark = jnp.where((iota((rows, 128), 1) == 0) & (live < 0.5), DEAD_MARK, found[:, :128])
        found = jnp.concatenate([mark, found[:, 128:]], axis=1).astype(BF16)
        src[r, pl.ds(first, steps)] = found.reshape(steps, block_slots, width)

    def send_part(r, q):
        each_step(
            q * quarter,
            (q + 1) * quarter,
            lambda i: pltpu.make_async_remote_copy(
                src_ref=src.at[r, i],
                dst_ref=dst.at[r, i],
                send_sem=send_sem.at[r],
                recv_sem=recv_sem.at[r, q],
                device_id=device(i),
                device_id_type=MESH,
            ).start(),
        )
        if q == 0:
            pltpu.make_async_copy(src.at[r, 0], dst.at[r, 0], recv_sem.at[r, 0]).start()

    def prepare(r):
        cent_copies[r].wait()
        corner = (iota((EXTRA, width), 0) == 0) & (iota((EXTRA, width), 1) == 0)
        cent[r, pl.ds(size, EXTRA)] = jnp.where(corner, 1.0, 0.0).astype(BF16)

        @pl.loop(0, size // 64)
        def _(b):
            rows = pl.ds(pl.multiple_of(b * 64, 64), 64)
            value = cent[r, rows].astype(F32)
            norm = jnp.sum(value * value, axis=1, keepdims=True)
            half_norm[r, rows] = jnp.broadcast_to(0.5 * norm, (64, 128))

    def assign(r, first, steps):
        rows = steps * block_slots
        for q in range(first // quarter, (first + steps) // quarter):
            landed = dst.at[r, pl.ds(q * quarter, quarter)]
            pltpu.make_async_copy(landed, landed, recv_sem.at[r, q]).wait()
        x = dst[r, pl.ds(first, steps)].reshape(rows, width)
        products = dot(cent[r], x, 1, 1)
        live = jnp.where(products[size : size + 1] < 0.75 * DEAD_MARK, 1.0, 0.0)
        norm = jnp.concatenate([half_norm[r]] * (rows // 128), axis=1)
        logits = (products[:size] - norm) * (sharp_ref[0, r] * width**-0.5)
        shifted = logits - jnp.max(logits, axis=0, keepdims=True)
        exponent = jnp.exp(shifted)
        total = jnp.sum(exponent, axis=0, keepdims=True)
        inverse_total = 1.0 / total
        entropy = jnp.log(total) - jnp.sum(exponent * shifted, axis=0, keepdims=True) * inverse_total
        weights = (exponent * (inverse_total * live)).astype(BF16)
        return x, weights, entropy

    def pack(r, first, entropy):
        held = lane // 32 == r
        for q in range(entropy.shape[1] // 128):
            row = entropy[:, 128 * q : 128 * (q + 1)]
            for g in range(4):
                at = 4 * (first // quarter + q) + g
                turn = (32 * (r - g)) % 128
                moved = pltpu.roll(row, turn, 1) if turn else row
                if r == 0:
                    packed[at] = moved
                else:
                    packed[at] = jnp.where(held, moved, packed[at])

    def weigh(r, first, x, weights):
        weighed = dot(weights, jnp.ones((x.shape[0], 128), BF16))
        weighted = dot(weights, x)
        if first == 0:
            mass[...] = weighed + PRIOR_MASS
            numer[...] = weighted + PRIOR_MASS * cent[r, pl.ds(0, size)].astype(F32)
        else:
            mass[...] += weighed
            numer[...] += weighted

    def member_of(r):
        own = parent[:, pl.ds(r * size, size)] - w * group
        return jnp.where(own == iota((group, size), 0), 1.0, 0.0).astype(BF16)

    def finish(r):
        member = member_of(r)
        high, low = split(mass[...])
        part_mass = dot(member, high) + dot(member, low)
        part_sum = dot(member, numer[...].astype(BF16))
        if r == 0:
            coarse_mass[...] = part_mass
            coarse[...] = part_sum
        else:
            coarse_mass[...] += part_mass
            coarse[...] += part_sum

    def emit(r):
        scale = 1.0 / mass[...]
        for d in range(width // 128):
            cols = pl.ds(128 * d, 128)
            fine_out[pl.ds(r * size, size), cols] = (numer[:, cols] * scale).astype(BF16)

    def whole_bucket(r):
        half = owners // 2
        for first in (0, half):
            x, weights, entropy = assign(r, first, half)
            pack(r, first, entropy)
            weigh(r, first, x, weights)
        finish(r)
        emit(r)

    gather_part(0, 0, quarter)
    pl.semaphore_wait(barrier, owners - 1)
    send_part(0, 0)
    sharp_copy = pltpu.make_async_copy(sharp_hbm, sharp_ref, load_sem.at[3])
    sharp_copy.start()
    parent_copy = pltpu.make_async_copy(parent_hbm, parent, load_sem.at[1])
    parent_copy.start()
    cent_copies = [
        pltpu.make_async_copy(
            fine_hbm.at[pl.ds(r * size, size)], cent.at[r, pl.ds(0, size)], cent_sem.at[r]
        )
        for r in range(buckets)
    ]
    for copy in cent_copies:
        copy.start()
    for q in range(1, 4):
        gather_part(0, q * quarter, quarter)
        send_part(0, q)
    for r in range(1, buckets):
        for q in (0, 2):
            gather_part(r, q * quarter, 2 * quarter)
            send_part(r, q)
            send_part(r, q + 1)
    sharp_copy.wait()
    parent_copy.wait()
    prepare(0)
    prepare(1)
    whole_bucket(0)
    prepare(2)
    whole_bucket(1)
    prepare(3)
    whole_bucket(2)

    def send_entropy(q):
        each_step(
            q * quarter,
            (q + 1) * quarter,
            lambda i: pltpu.make_async_remote_copy(
                src_ref=packed.at[lax.div(i, 8)],
                dst_ref=back.at[i],
                send_sem=ent_sem.at[0],
                recv_sem=ent_sem.at[1],
                device_id=source(i),
                device_id_type=MESH,
            ).start(),
        )
        if q == 0:
            pltpu.make_async_copy(packed.at[0], back.at[0], ent_sem.at[1]).start()

    for q in range(3):
        x, weights, entropy = assign(last, q * quarter, quarter)
        pack(last, q * quarter, entropy)
        send_entropy(q)
        weigh(last, q * quarter, x, weights)
    finish(last)

    member = member_of(last)
    x, weights, entropy = assign(last, 3 * quarter, quarter)
    shares = dot(member, weights)
    coarse_mass[...] += jnp.sum(shares, axis=1, keepdims=True)
    shares = shares.astype(BF16)

    y, core = lax.div(n, 2), lax.rem(n, 2)
    ys = narrow // 2
    own_rows = group // narrow
    half = width // 2
    core_sends, core_recvs = (core_send0, core_send1), (core_recv0, core_recv1)
    y_sends, y_recvs = (y_send0, y_send1), (y_recv0, y_recv1)

    def tile_of(value):
        high, low = split(value)
        return jnp.where(iota((own_rows, 128), 1) < 64, high.astype(F32), low.astype(F32)).astype(BF16)

    def whole_of(value):
        value = value.astype(F32)
        return value + pltpu.roll(value, 64, 1)

    def rows_of(k, c):
        return pl.ds(pl.multiple_of((2 * k + c) * own_rows, own_rows), own_rows)

    core_copies = []
    for h in range(2):
        cols = pl.ds(h * half, half)
        coarse[:, cols] += dot(shares, x[:, h * half : (h + 1) * half])
        for k in range(ys):
            rows = rows_of(k, 1 - core)
            core_sends[h][k, :, pl.ds(0, half)] = coarse[rows, cols].astype(BF16)
            if h == 0:
                core_sends[h][k, :, pl.ds(half, 128)] = tile_of(coarse_mass[rows])
        copy = pltpu.make_async_remote_copy(
            src_ref=core_sends[h],
            dst_ref=core_recvs[h],
            send_sem=core_send_sem.at[h],
            recv_sem=core_recv_sem.at[h],
            device_id=(w, n + 1 - 2 * core),
            device_id_type=MESH,
        )
        copy.start()
        core_copies.append(copy)
    pack(last, 3 * quarter, entropy)
    send_entropy(3)

    def chip_sum(h, k):
        cols = pl.ds(h * half, half)
        rows = rows_of(k, core)
        return coarse[rows, cols] + core_recvs[h][k, :, pl.ds(0, half)].astype(F32)

    def chip_mass(k):
        return coarse_mass[rows_of(k, core)] + whole_of(core_recv0[k, :, pl.ds(half, 128)])

    y_copies = []
    for h in range(2):
        core_copies[h].wait()
        for k in (2, 1, 3):
            other = lax.rem(y + k, ys)
            y_sends[h][k - 1, :, pl.ds(0, half)] = chip_sum(h, other).astype(BF16)
            if h == 0:
                y_sends[h][k - 1, :, pl.ds(half, 128)] = tile_of(chip_mass(other))
            copy = pltpu.make_async_remote_copy(
                src_ref=y_sends[h].at[k - 1],
                dst_ref=y_recvs[h].at[k - 1],
                send_sem=y_send_sem.at[h, k - 1],
                recv_sem=y_recv_sem.at[h, k - 1],
                device_id=(w, 2 * other + core),
                device_id_type=MESH,
            )
            copy.start()
            y_copies.append(copy)
    weigh(last, 3 * quarter, x, weights)
    emit(last)
    total = [chip_sum(h, y) for h in range(2)]
    weight = chip_mass(y)
    for h in range(2):
        for k in range(ys - 1):
            y_copies[h * (ys - 1) + k].wait()
        for k in range(ys - 1):
            total[h] = total[h] + y_recvs[h][k, :, pl.ds(0, half)].astype(F32)
            if h == 0:
                weight = weight + whole_of(y_recv0[k, :, pl.ds(half, 128)])
        total_out[:, pl.ds(h * half, half)] = total[h]
    weight_out[...] = weight
    pltpu.make_async_copy(back, back, ent_sem.at[1]).wait()
    back_out[...] = back[...].reshape(owners, 128)

    for r in range(buckets):
        sent = src.at[r, pl.ds(0, owners - 1)]
        pltpu.make_async_copy(sent, sent, send_sem.at[r]).wait()
    sent = back.at[pl.ds(0, owners - 1)]
    pltpu.make_async_copy(sent, sent, ent_sem.at[0]).wait()


def close(
    fine, total, weight, code, back, old, fine_out, coarse_out, entropy_out, coarse, point, sem
):
    fine_copy = pltpu.make_async_copy(fine, fine_out, sem.at[0])
    fine_copy.start()
    scale = 0.5 / (weight[...] + PRIOR_MASS)
    for d in range(total.shape[1] // 128):
        cols = pl.ds(128 * d, 128)
        coarse[:, cols] = (0.5 * old[:, cols].astype(F32) + total[:, cols] * scale).astype(BF16)
    coarse_copy = pltpu.make_async_copy(coarse, coarse_out, sem.at[1])
    coarse_copy.start()
    owners, n_points = back.shape[0], code.shape[1]
    high, low = split(back[...])
    number = code[...]
    place = lax.shift_right_logical(number, 2) & (owners - 1)
    hot = jnp.where(place == iota((owners, n_points), 0), 1.0, 0.0).astype(BF16)
    found = dot(high, hot, 0, 0) + dot(low, hot, 0, 0)
    spot = 32 * lax.shift_right_logical(number, 9) + (number & 31)
    mine = spot == iota((128, n_points), 0)
    point[...] = jnp.sum(jnp.where(mine, found, 0.0), axis=0, keepdims=True)
    point_copy = pltpu.make_async_copy(point, entropy_out, sem.at[2])
    point_copy.start()
    coarse_copy.wait()
    point_copy.wait()
    fine_copy.wait()


def body(points, block_bucket, fine, sharp, parents, coarse_old):
    wide, narrow = lax.axis_size("wide"), lax.axis_size("narrow")
    owners = wide * narrow
    n_points, width = points.shape
    n_blocks = block_bucket.shape[0]
    buckets = sharp.shape[0]
    size = fine.shape[0] // buckets
    block_slots = CAP * (n_points // n_blocks)
    own_rows = coarse_old.shape[0]
    group = own_rows * narrow
    ys = narrow // 2
    half = width // 2
    whole = pl.BlockSpec(memory_space=pltpu.VMEM)
    anywhere = pl.BlockSpec(memory_space=pl.ANY)
    in_hbm = pl.BlockSpec(memory_space=pltpu.HBM)
    dma = pltpu.SemaphoreType.DMA
    held = pl.pallas_call(
        functools.partial(kernel, (wide, narrow)),
        out_shape=(
            pltpu.VMEM(fine.shape, BF16),
            pltpu.VMEM(coarse_old.shape, F32),
            pltpu.VMEM((own_rows, 128), F32),
            pltpu.VMEM((1, n_points), jnp.int32),
            pltpu.VMEM((owners, 128), F32),
        ),
        in_specs=[in_hbm] * 5,
        out_specs=(whole,) * 5,
        scratch_shapes=[
            pltpu.SMEM((1, buckets), F32),
            pltpu.VMEM((1, n_blocks), jnp.int32),
            pltpu.VMEM((n_points, width), BF16),
            pltpu.VMEM((buckets, size + EXTRA, width), BF16),
            pltpu.VMEM((buckets, size, 128), F32),
            pltpu.VMEM((1, buckets * size), jnp.int32),
            pltpu.VMEM((buckets, owners, block_slots, width), BF16),
            pltpu.VMEM((buckets, owners, block_slots, width), BF16),
            pltpu.VMEM((size, width), F32),
            pltpu.VMEM((size, 128), F32),
            pltpu.VMEM((group, width), F32),
            pltpu.VMEM((group, 128), F32),
            pltpu.VMEM((owners // 8, 1, 128), F32),
            pltpu.VMEM((owners, 1, 128), F32),
            pltpu.VMEM((ys, own_rows, half + 128), BF16),
            pltpu.VMEM((ys, own_rows, half), BF16),
            pltpu.VMEM((ys, own_rows, half + 128), BF16),
            pltpu.VMEM((ys, own_rows, half), BF16),
            pltpu.VMEM((ys - 1, own_rows, half + 128), BF16),
            pltpu.VMEM((ys - 1, own_rows, half), BF16),
            pltpu.VMEM((ys - 1, own_rows, half + 128), BF16),
            pltpu.VMEM((ys - 1, own_rows, half), BF16),
            dma((4,)),
            dma((buckets,)),
            dma((buckets,)),
            dma((buckets, 4)),
            dma((2,)),
            dma((2,)),
            dma((2,)),
            dma((2, ys - 1)),
            dma((2, ys - 1)),
        ],
        compiler_params=pltpu.CompilerParams(
            collective_id=0, has_side_effects=True, vmem_limit_bytes=48 << 20
        ),
    )(
        *[
            pltpu.with_memory_space_constraint(value, pltpu.HBM)
            for value in (
                sharp.reshape(1, buckets),
                block_bucket.reshape(1, n_blocks),
                parents.reshape(1, buckets * size),
                points,
                fine,
            )
        ],
    )
    fine_new, coarse_new, entropy = pl.pallas_call(
        close,
        out_shape=(
            jax.ShapeDtypeStruct(fine.shape, BF16),
            jax.ShapeDtypeStruct(coarse_old.shape, BF16),
            jax.ShapeDtypeStruct((1, n_points), F32),
        ),
        in_specs=[whole] * 6,
        out_specs=(anywhere,) * 3,
        scratch_shapes=[
            pltpu.VMEM(coarse_old.shape, BF16),
            pltpu.VMEM((1, n_points), F32),
            dma((3,)),
        ],
        compiler_params=pltpu.CompilerParams(vmem_limit_bytes=16 << 20),
    )(*[pltpu.with_memory_space_constraint(value, pltpu.VMEM) for value in (*held, coarse_old)])
    return fine_new, coarse_new, entropy.reshape(n_points)


def solution(mesh):
    both = ("wide", "narrow")
    return jax.shard_map(
        body,
        mesh=mesh,
        in_specs=(P(both, None), P(both), P(both, None), P(both), P(both), P(both, None)),
        out_specs=(P(both, None), P(both, None), P(both)),
        check_vma=False,
    )
```
